128 devices in a mesh: row: 8 (over y, z_hi), col: 16 (over x, z_lo, core).
Axes of the slice: x: 4, y: 4, z: 4 (z_hi: 2, z_lo: 2; z = z_hi * 2 + z_lo), core: 2. Of those that a mesh axis runs over, the one named last changes fastest.
Arguments:
- samples: bfloat16 [8192, 8192], P('col'), may hold values from -6 to 6
- shrink: float32 [8192], replicated, may hold values from 0.5 to 2
Outputs:
- factored: float32 [8, 1024, 16, 512], P('row', None, 'col')
The draws below stay inside these ranges and needn't reach their ends.
All inputs are finite; a program needn't handle non-finite values.
Results may differ from the reference program's by a relative error of at most 0.0003.
Values may be sent and summed in bfloat16 or wider, within the bound.
No kernel may reach another device: no remote copies, remote signals or barrier semaphores. Data moves between devices by JAX's collectives and lax.ppermute only.
A program may use at most 128 MiB of HBM per device.

```python
import math
import jax
import jax.numpy as jnp
from jax import lax

P_SIZE = 8192
COL_BLOCK = 256
PANEL = 512
ROW_DEVS = 8
COL_DEVS = 16
NTOT = 8192
ROW_BLOCK = 64


def levels(stream_key, extent, pieces, smallest, high):
    loudness, own = 1.0, jax.random.fold_in(stream_key, 6)
    for dim, shards_of in pieces:
        draws = jnp.exp(jax.random.uniform(jax.random.fold_in(own, dim), (shards_of,), jnp.float32, smallest / len(pieces), high / len(pieces)))
        loudness = loudness * jnp.repeat(draws, extent[dim] // shards_of).reshape([-1 if axis == dim else 1 for axis in range(len(extent))])
    return loudness


def normal_values(stream_key, shape, width, reach, cuts=(), dtype=jnp.bfloat16):
    result = jax.random.normal(stream_key, shape, jnp.float32) * width
    if len(cuts) > 0:
        result = levels(stream_key, shape, cuts, -0.22, 0.18) * result
    return jnp.clip(result, min=-reach, max=reach).astype(dtype)


def setup_inputs(seed: int = 0) -> dict:
    key_of = jax.random.split(jax.random.key(seed), 3)
    samples = normal_values(key_of[0], (NTOT, P_SIZE), 1.0, 6.0, ((0, 16),))
    shrink = jnp.clip(jnp.exp(jax.random.uniform(key_of[1], (P_SIZE,), jnp.float32, math.log(0.5), math.log(2.0))), 0.5, 2.0)
    return dict(samples=samples, shrink=shrink)


def reference(samples, shrink):
    gram = jnp.dot(samples.T.astype(jnp.float32), samples.astype(jnp.float32), preferred_element_type=jnp.float32)
    covariance = gram / jnp.float32(NTOT) + jnp.diag(shrink)
    leading = jnp.linalg.cholesky(covariance[:PANEL, :PANEL])
    panel_factor = lax.linalg.triangular_solve(leading, covariance[:, :PANEL].T, left_side=True, lower=True).T
    upper_solve = lax.linalg.triangular_solve(leading, covariance[:PANEL, :], left_side=True, lower=True)
    updated = covariance - jnp.dot(panel_factor.astype(jnp.float32), upper_solve.astype(jnp.float32), precision=lax.Precision.HIGHEST, preferred_element_type=jnp.float32)
    updated = updated.at[:, :PANEL].set(panel_factor)
    row_groups = P_SIZE // (ROW_DEVS * ROW_BLOCK)
    col_groups = P_SIZE // (COL_DEVS * COL_BLOCK)
    arranged = updated.reshape(row_groups, ROW_DEVS, ROW_BLOCK, col_groups, COL_DEVS, COL_BLOCK)
    arranged = arranged.transpose(1, 0, 2, 4, 3, 5)
    return arranged.reshape(ROW_DEVS, P_SIZE // ROW_DEVS, COL_DEVS, P_SIZE // COL_DEVS)
```

```python
import jax
import jax.numpy as jnp
import numpy as np
from jax import lax
from jax.experimental import pallas as pl
from jax.experimental.pallas import tpu as pltpu
from jax.sharding import Mesh, PartitionSpec as P

PANEL = 512
VARS = 8192
ROWS = 512
HI = lax.Precision.HIGHEST
F32 = jnp.float32
BF = jnp.bfloat16
MB = 1 << 20
ANY = pl.BlockSpec(memory_space=pl.ANY)
VM = pl.BlockSpec(memory_space=pltpu.VMEM)


def params(mb):
    return pltpu.CompilerParams(vmem_limit_bytes=mb * MB)


def nt(a, b, precision=None):
    return lax.dot_general(
        a, b, (((1,), (1,)), ((), ())), precision=precision, preferred_element_type=F32
    )


def nn(a, b, precision=None):
    return lax.dot_general(
        a, b, (((1,), (0,)), ((), ())), precision=precision, preferred_element_type=F32
    )


def prep_kernel(x_ref, rows_ref, lead_ref):
    r = lax.axis_index("y") * 2 + lax.axis_index("zh")
    i = lax.broadcasted_iota(jnp.int32, (64, 512), 0)
    j = lax.broadcasted_iota(jnp.int32, (64, 512), 1)
    pick = jnp.where(j == r * 64 + i, 1.0, 0.0).astype(BF)
    for h in range(2):
        rows_ref[h * 64 : h * 64 + 64, :] = nt(pick, x_ref[:, h * 512 : h * 512 + 512]).astype(BF)

    @pl.when(pl.program_id(0) == 0)
    def _():
        a = lax.broadcasted_iota(jnp.int32, (512, 512), 0)
        b = lax.broadcasted_iota(jnp.int32, (512, 512), 1)
        eye = jnp.where(a == b, 1.0, 0.0).astype(BF)
        lead_ref[...] = nt(eye, x_ref[:, :512]).astype(BF)


def prep(x):
    return pl.pallas_call(
        prep_kernel,
        grid=(8,),
        in_specs=[pl.BlockSpec((ROWS, 1024), lambda g: (0, g))],
        out_specs=[
            pl.BlockSpec((128, ROWS), lambda g: (g, 0)),
            pl.BlockSpec((512, ROWS), lambda g: (0, 0)),
        ],
        out_shape=[
            jax.ShapeDtypeStruct((1024, ROWS), BF),
            jax.ShapeDtypeStruct((512, ROWS), BF),
        ],
        compiler_params=params(24),
        cost_estimate=pl.CostEstimate(flops=2 << 30, bytes_accessed=10 * MB, transcendentals=0),
        name="prep",
    )(x)


def lead_kernel(*refs):
    pieces, out = refs[:-1], refs[-1]
    total = None
    values = []
    for z in range(0, len(pieces), 5):
        values += [p[...] for p in pieces[z : z + 3]]
        values.append(jnp.concatenate([p[...] for p in pieces[z + 3 : z + 5]], axis=0))
    for v in values:
        term = nt(v, v)
        total = term if total is None else total + term
    out[...] = total


def lead_gram(pieces):
    return pl.pallas_call(
        lead_kernel,
        in_specs=[VM] * len(pieces),
        out_specs=VM,
        out_shape=jax.ShapeDtypeStruct((512, 512), F32),
        compiler_params=params(24),
        cost_estimate=pl.CostEstimate(flops=2 << 30, bytes_accessed=6 * MB, transcendentals=0),
        name="lead_gram",
    )(*pieces)


def factor128(block):
    tiles = [block[8 * t : 8 * t + 8, :] for t in range(16)]
    lane = lax.broadcasted_iota(jnp.int32, (8, 128), 1)
    sub = lax.broadcasted_iota(jnp.int32, (8, 128), 0)
    for j in range(128):
        t0, s = j // 8, j % 8
        row = tiles[t0][s : s + 1, :]
        inv = 1.0 / row[:, j : j + 1]
        at = lane == j
        rowc = jnp.where(at[:1], inv, row * inv)
        for t in range(t0, 16):
            col = tiles[t][:, j : j + 1]
            base = jnp.where(at, 0.0, tiles[t])
            if t == t0:
                below = sub > s
                new = base - col * rowc
                tiles[t] = jnp.where(below, new, tiles[t])
            else:
                tiles[t] = base - col * rowc
    whole = jnp.concatenate(tiles, axis=0)
    a = lax.broadcasted_iota(jnp.int32, (128, 128), 0)
    b = lax.broadcasted_iota(jnp.int32, (128, 128), 1)
    d = jnp.sum(jnp.where(a == b, whole, 0.0), axis=1, keepdims=True)
    rs = 1.0 / jnp.sqrt(d)
    return jnp.where(a > b, whole * rs, jnp.where(a == b, rs, 0.0))


def chol_kernel(g0, g1, shrink_ref, inv_ref, a_ref):
    i = lax.broadcasted_iota(jnp.int32, (512, 512), 0)
    j = lax.broadcasted_iota(jnp.int32, (512, 512), 1)
    a_ref[...] = (g0[...] + g1[...]) * F32(1.0 / VARS) + jnp.where(
        i == j, shrink_ref[...], 0.0
    )
    inv_ref[...] = jnp.zeros((512, 512), F32)
    for b in range(4):
        lo, hi = b * 128, b * 128 + 128
        w = factor128(a_ref[lo:hi, lo:hi])
        if b > 0:
            mid = nn(a_ref[lo:hi, :lo], inv_ref[:lo, :lo], HI)
            inv_ref[lo:hi, :lo] = -nn(w, mid, HI)
        inv_ref[lo:hi, lo:hi] = w
        if b < 3:
            below = nt(a_ref[hi:, lo:hi], w, HI)
            a_ref[hi:, lo:hi] = below
            a_ref[hi:, hi:] = a_ref[hi:, hi:] - nt(below, below, HI)


def chol_inverse(g0, g1, shrink_lead):
    return pl.pallas_call(
        chol_kernel,
        in_specs=[VM] * 3,
        out_specs=VM,
        out_shape=jax.ShapeDtypeStruct((512, 512), F32),
        scratch_shapes=[pltpu.VMEM((512, 512), F32)],
        compiler_params=params(16),
        cost_estimate=pl.CostEstimate(flops=40 << 30, bytes_accessed=3 * MB, transcendentals=0),
        name="chol_inverse",
    )(g0, g1, shrink_lead)


def gram_kernel(n_a, n_l, *refs):
    a_in, l_in, b_in = refs[:n_a], refs[n_a : n_a + n_l], refs[n_a + n_l : -9]
    own, other, rl, lc_own, lc_other = refs[-9:-4]
    a_s, l_s, b_s, sems = refs[-4:]
    y, zh = lax.axis_index("y"), lax.axis_index("zh")
    x, zl = lax.axis_index("x"), lax.axis_index("zl")
    copies = []

    def put(src, dst):
        c = pltpu.make_async_copy(src, dst, sems.at[len(copies)])
        c.start()
        copies.append(c)

    def lanes(dx, dz):
        k = lax.rem(x + dx, 4) * 2 + lax.rem(zl + dz, 2)
        return pl.ds(pl.multiple_of(k * 512, 512), 512)

    for refs_in, scratch, rows in ((a_in, a_s, 1024), (l_in, l_s, 512)):
        at = 0
        for dz in range(2):
            for dx in (0, 1, 3):
                put(refs_in[at], scratch.at[:, lanes(dx, dz)])
                at += 1
            for h in range(2):
                part = pl.ds(h * (rows // 2), rows // 2)
                put(refs_in[at], scratch.at[part, lanes(2, dz)])
                at += 1
    at = 0
    for dz in range(2):
        for dy in (0, 1, 3):
            r = lax.rem(y + dy, 4) * 2 + lax.rem(zh + dz, 2)
            put(b_in[at], b_s.at[:, r])
            at += 1
        for h in range(2):
            r = lax.rem(y + 2, 4) * 2 + lax.rem(zh + dz, 2)
            put(b_in[at], b_s.at[pl.ds(h * 4, 4), r])
            at += 1
    for c in copies:
        c.wait()

    def product(left):
        total = None
        for k in range(8):
            term = nn(left[:, k * 512 : k * 512 + 512], b_s[k].reshape(512, 1024))
            total = term if total is None else total + term
        return total

    def lead_step(m, _):
        rows = pl.ds(pl.multiple_of(m * 256, 256), 256)
        out = product(l_s[rows, :])
        lc_own[rows, :] = out[:, :512]
        lc_other[rows, :] = out[:, 512:]
        return 0

    def row_step(m, _):
        rows = pl.ds(pl.multiple_of(m * 256, 256), 256)
        left = a_s[rows, :]
        rl[rows, :] = nt(left, l_s[...])
        out = product(left)
        own[rows, :] = out[:, :512]
        other[rows, :] = out[:, 512:]
        return 0

    lax.fori_loop(0, 2, lead_step, 0)
    lax.fori_loop(0, 4, row_step, 0)


def gram(a, l, b):
    n = len(a) + len(l) + len(b)

    def body(*refs):
        gram_kernel(len(a), len(l), *refs)

    return pl.pallas_call(
        body,
        in_specs=[ANY] * n,
        out_specs=[VM] * 5,
        out_shape=[
            jax.ShapeDtypeStruct((1024, 512), F32),
            jax.ShapeDtypeStruct((1024, 512), F32),
            jax.ShapeDtypeStruct((1024, 512), F32),
            jax.ShapeDtypeStruct((512, 512), F32),
            jax.ShapeDtypeStruct((512, 512), F32),
        ],
        scratch_shapes=[
            pltpu.VMEM((1024, 4096), BF),
            pltpu.VMEM((512, 4096), BF),
            pltpu.VMEM((8, 8, 64, 1024), BF),
            pltpu.SemaphoreType.DMA((n,)),
        ],
        compiler_params=params(52),
        cost_estimate=pl.CostEstimate(flops=17 << 30, bytes_accessed=28 * MB, transcendentals=0),
        name="gram",
    )(*a, *l, *b)


def final_kernel(tm, tr, rm, rr, lm, lr, inv_ref, sl_ref, sc_ref, out_ref, u_ref):
    r = lax.axis_index("y") * 2 + lax.axis_index("zh")
    k = lax.axis_index("x") * 2 + lax.axis_index("zl")
    core = lax.axis_index("core")
    step = pl.program_id(0)
    scale = F32(1.0 / VARS)
    lane = lax.broadcasted_iota(jnp.int32, (512, 512), 1)
    col = (lane // 256) * 4096 + k * 512 + core * 256 + lane % 256

    @pl.when(step == 0)
    def _():
        row = lax.broadcasted_iota(jnp.int32, (512, 512), 0)
        c = (lm[...] + lr[...]) * scale + jnp.where(row == col, sc_ref[...], 0.0)
        u_ref[...] = nn(inv_ref[...], c, HI)

    local = lax.broadcasted_iota(jnp.int32, (256, 512), 0) + step * 256
    row = (local // 64) * 512 + r * 64 + local % 64
    lead = lax.broadcasted_iota(jnp.int32, (256, 512), 1)
    c_rl = (rm[...] + rr[...]) * scale + jnp.where(row == lead, sl_ref[...], 0.0)
    panel = nt(c_rl, inv_ref[...], HI)
    c = (tm[...] + tr[...]) * scale + jnp.where(row == col[:256], sc_ref[...], 0.0)
    out_ref[...] = c - nn(panel, u_ref[...], HI)

    @pl.when(k == 0)
    def _():
        out_ref[:, :256] = jnp.where(core == 0, panel[:, :256], panel[:, 256:])


def final(tm, tr, rm, rr, lm, lr, inv, sl, sc):
    block = pl.BlockSpec((256, 512), lambda m: (m, 0))
    full = pl.BlockSpec((512, 512), lambda m: (0, 0))
    line = pl.BlockSpec((1, 512), lambda m: (0, 0))
    return pl.pallas_call(
        final_kernel,
        grid=(4,),
        in_specs=[block] * 4 + [full] * 3 + [line] * 2,
        out_specs=block,
        out_shape=jax.ShapeDtypeStruct((1024, 512), F32),
        scratch_shapes=[pltpu.VMEM((512, 512), F32)],
        compiler_params=params(32),
        cost_estimate=pl.CostEstimate(flops=8 << 30, bytes_accessed=14 * MB, transcendentals=0),
        name="final",
    )(tm, tr, rm, rr, lm, lr, inv, sl, sc)


def shift(v, axis, by):
    n = lax.axis_size(axis)
    return lax.ppermute(v, axis, [(i, (i + by) % n) for i in range(n)])


def ring(v, axis):
    below = shift(v, axis, 1)
    above = shift(v, axis, -1)
    half = v.shape[0] // 2
    return [v, above, below, shift(below[:half], axis, 1), shift(above[half:], axis, -1)]


def body(samples, shrink):
    r = lax.axis_index("y") * 2 + lax.axis_index("zh")
    k = lax.axis_index("x") * 2 + lax.axis_index("zl")
    core = lax.axis_index("core")
    rows_t, lead_t = prep(samples)
    strip = lax.dynamic_slice_in_dim(samples, r * 64, 64, 0).reshape(64, 2, 8, 2, 256)
    strip = strip.transpose(2, 0, 3, 1, 4)
    strip = jnp.where(core == 0, strip, strip[:, :, ::-1]).reshape(8, 64, 1024)

    lead_z = shift(lead_t, "zl", 1)
    lead = ring(lead_t, "x") + ring(lead_z, "x")
    cols = lax.all_to_all(strip, ("x", "zl"), split_axis=0, concat_axis=0, tiled=True)
    cols_z = shift(cols, "zh", 1)
    rows_z = shift(rows_t, "zl", 1)
    a = ring(rows_t, "x") + ring(rows_z, "x")
    b = ring(cols, "y") + ring(cols_z, "y")

    g = lead_gram(lead)
    sl = shrink[:PANEL].reshape(1, PANEL)
    inv = chol_inverse(g, shift(g, "core", 1), sl)
    own, other, rl, lc_own, lc_other = gram(a, lead, b)
    sc = lax.dynamic_slice(shrink.reshape(2, 16, 256), (0, 2 * k + core, 0), (2, 1, 256))
    out = final(
        own, shift(other, "core", 1),
        rl, shift(rl, "core", 1),
        lc_own, shift(lc_other, "core", 1),
        inv, sl, sc.reshape(1, 512),
    )
    return out.reshape(1, 1024, 1, 512)


def solution(mesh):
    fine = Mesh(mesh.devices.reshape(4, 2, 4, 2, 2), ("y", "zh", "x", "zl", "core"))
    return jax.shard_map(
        body,
        mesh=fine,
        in_specs=(P(("x", "zl", "core"), None), P()),
        out_specs=P(("y", "zh"), None, ("x", "zl", "core"), None),
        check_vma=False,
    )
```

```python
import jax
import jax.numpy as jnp
from jax import lax
from jax.experimental import pallas as pl
from jax.experimental.pallas import tpu as pltpu
from jax.sharding import Mesh, PartitionSpec as P

PANEL = 512
VARS = 8192
ROWS = 512
HI = lax.Precision.HIGHEST
F32 = jnp.float32
BF = jnp.bfloat16
MB = 1 << 20


def cost(us):
    return pl.CostEstimate(flops=us << 30, bytes_accessed=1 << 16, transcendentals=0)


ANY = pl.BlockSpec(memory_space=pl.ANY)
VM = pl.BlockSpec(memory_space=pltpu.VMEM)


def params(mb):
    return pltpu.CompilerParams(vmem_limit_bytes=mb * MB)


def nt(a, b, precision=None):
    return lax.dot_general(
        a, b, (((1,), (1,)), ((), ())), precision=precision, preferred_element_type=F32
    )


def nn(a, b, precision=None):
    return lax.dot_general(
        a, b, (((1,), (0,)), ((), ())), precision=precision, preferred_element_type=F32
    )


def prep_kernel(lo_ref, hi_ref, rows_ref, up_ref, down_ref, lead_ref, strip_ref, pick_ref):
    y, zh, zl = lax.axis_index("y"), lax.axis_index("zh"), lax.axis_index("zl")
    r = y * 2 + zh
    core = lax.axis_index("core")
    @pl.when(pl.program_id(0) == 0)
    def _():
        j = lax.broadcasted_iota(jnp.int32, (512, 128), 0)
        i = lax.broadcasted_iota(jnp.int32, (512, 128), 1)
        for h, by in enumerate((1, 3)):
            other = y * 2 + lax.rem(zh * 2 + zl + by, 4) // 2
            want = jnp.where(i < 64, r * 64 + i, other * 64 + i - 64)
            pick_ref[h] = jnp.where(j == want, 1.0, 0.0).astype(BF)

    mine = pl.ds(pl.multiple_of((zh * 4 + y) * 64, 64), 64)
    for h, (ref, out) in enumerate(((lo_ref, up_ref), (hi_ref, down_ref))):
        picked = nn(ref[...], pick_ref[h]).astype(BF).T
        rows_ref[h, 0] = picked[:64]
        out[0] = picked[64:]
        part = ref[mine, :]
        left, right = part[:, :256], part[:, 256:]
        strip_ref[0, :, h * 256 : h * 256 + 256] = jnp.where(core == 0, left, right)
        strip_ref[0, :, 512 + h * 256 : 768 + h * 256] = jnp.where(core == 0, right, left)

    @pl.when(pl.program_id(0) == 0)
    def _():
        lead_ref[...] = lo_ref[...].T


def prep(x):
    rows, up, down, lead, strip = pl.pallas_call(
        prep_kernel,
        grid=(8,),
        in_specs=[
            pl.BlockSpec((ROWS, 512), lambda k: (0, k)),
            pl.BlockSpec((ROWS, 512), lambda k: (0, k + 8)),
        ],
        out_specs=[
            pl.BlockSpec((2, 1, 64, ROWS), lambda k: (0, k, 0, 0)),
            pl.BlockSpec((1, 64, ROWS), lambda k: (k, 0, 0)),
            pl.BlockSpec((1, 64, ROWS), lambda k: (k, 0, 0)),
            pl.BlockSpec((512, ROWS), lambda k: (0, 0)),
            pl.BlockSpec((1, 64, 1024), lambda k: (k, 0, 0)),
        ],
        out_shape=[
            jax.ShapeDtypeStruct((2, 8, 64, ROWS), BF),
            jax.ShapeDtypeStruct((8, 64, ROWS), BF),
            jax.ShapeDtypeStruct((8, 64, ROWS), BF),
            jax.ShapeDtypeStruct((512, ROWS), BF),
            jax.ShapeDtypeStruct((8, 64, 1024), BF),
        ],
        scratch_shapes=[pltpu.VMEM((2, 512, 128), BF)],
        compiler_params=params(58),
        cost_estimate=cost(9),
        name="prep",
    )(x, x)
    return rows.reshape(1024, ROWS), up.reshape(512, ROWS), down.reshape(512, ROWS), lead, strip


def place(dx, dz):
    return lax.rem(lax.axis_index("x") + dx, 4) * 2 + lax.rem(lax.axis_index("zl") + dz, 2)


def lead_kernel(*refs):
    gram_ref, all_ref = refs[-2:]
    for dz in range(2):
        for n, dx in enumerate((0, 1, 3, 2)):
            all_ref[place(dx, dz)] = refs[4 * dz + n][...]
    total = None
    for k in range(8):
        v = all_ref[k]
        term = nt(v, v)
        total = term if total is None else total + term
    gram_ref[...] = total


def lead_gram(pieces):
    return pl.pallas_call(
        lead_kernel,
        in_specs=[VM] * len(pieces),
        out_specs=[VM, VM],
        out_shape=[
            jax.ShapeDtypeStruct((512, 512), F32),
            jax.ShapeDtypeStruct((8, 512, 512), BF),
        ],
        compiler_params=params(24),
        cost_estimate=cost(4),
        name="lead_gram",
    )(*pieces)


def factor128(block):
    tiles = [block[8 * t : 8 * t + 8, :] for t in range(16)]
    lane = lax.broadcasted_iota(jnp.int32, (8, 128), 1)
    sub = lax.broadcasted_iota(jnp.int32, (8, 128), 0)
    out = []
    for g in range(16):
        j0 = 8 * g
        group = (lane >= j0) & (lane < j0 + 8)
        cols = [jnp.broadcast_to(tiles[g][:, j0 + s : j0 + s + 1], (8, 128)) for s in range(8)]
        jordan = jnp.where(group, jnp.where(lane - j0 == sub, 1.0, 0.0), tiles[g])
        kept = jnp.zeros((8, 128), F32)
        invs = jnp.ones((8, 128), F32)
        for s in range(8):
            here = sub == s
            inv = 1.0 / jnp.broadcast_to(cols[s][s : s + 1, :], (8, 128))
            row = jnp.broadcast_to(jordan[s : s + 1, :], (8, 128))
            kept = jnp.where(here, row, kept)
            invs = jnp.where(here, inv, invs)
            factor = jnp.where(here, 1.0 - inv, cols[s] * inv)
            jordan = jordan - factor * row
            for q in range(s + 1, 8):
                cols[q] = cols[q] - factor * jnp.broadcast_to(cols[q][s : s + 1, :], (8, 128))
        out.append(jnp.where(lane <= sub + j0, kept * jnp.sqrt(invs), 0.0))
        for t in range(g + 1, 16):
            tile = jnp.where(group, 0.0, tiles[t])
            for s in range(8):
                tile = tile - tiles[t][:, j0 + s : j0 + s + 1] * jordan[s : s + 1, :]
            tiles[t] = tile
    return jnp.concatenate(out, axis=0)


def chol_blocks(a_ref, inv_ref, blocks):
    for b in blocks:
        lo, hi = b * 128, b * 128 + 128
        w = factor128(a_ref[lo:hi, lo:hi])
        if b > 0:
            mid = nn(a_ref[lo:hi, :lo], inv_ref[:lo, :lo], HI)
            inv_ref[lo:hi, :lo] = -nn(w, mid, HI)
        inv_ref[lo:hi, lo:hi] = w
        if b < 3:
            below = nt(a_ref[hi:, lo:hi], w, HI)
            a_ref[hi:, lo:hi] = below
            a_ref[hi:, hi:] = a_ref[hi:, hi:] - nt(below, below, HI)


def chol_first(g0, g1, shrink_ref, a_ref, inv_ref):
    i = lax.broadcasted_iota(jnp.int32, (512, 512), 0)
    j = lax.broadcasted_iota(jnp.int32, (512, 512), 1)
    a_ref[...] = (g0[...] + g1[...]) * F32(1.0 / VARS) + jnp.where(
        i == j, shrink_ref[...], 0.0
    )
    inv_ref[...] = jnp.zeros((512, 512), F32)
    chol_blocks(a_ref, inv_ref, (0, 1))


def chol_second(a0, i0, inv_ref, a_ref):
    a_ref[...] = a0[...]
    inv_ref[...] = i0[...]
    chol_blocks(a_ref, inv_ref, (2, 3))


SQUARE = jax.ShapeDtypeStruct((512, 512), F32)


def chol_half(g0, g1, shrink_lead):
    return pl.pallas_call(
        chol_first,
        in_specs=[VM] * 3,
        out_specs=[VM, VM],
        out_shape=[SQUARE, SQUARE],
        compiler_params=params(16),
        cost_estimate=cost(80),
        name="chol_first",
    )(g0, g1, shrink_lead)


def chol_rest(a, inv):
    return pl.pallas_call(
        chol_second,
        in_specs=[VM, VM],
        out_specs=VM,
        out_shape=SQUARE,
        scratch_shapes=[pltpu.VMEM((512, 512), F32)],
        compiler_params=params(16),
        cost_estimate=cost(80),
        name="chol_second",
    )(a, inv)


TALL = jax.ShapeDtypeStruct((1024, 512), F32)
ORDER = tuple((dx, dz) for dz in range(2) for dx in (0, 1, 3, 2))


def fetch(b_ref, b_s, sems):
    copies = []
    for y in range(4):
        c = pltpu.make_async_copy(b_ref.at[y], b_s.at[:, y], sems.at[y])
        c.start()
        copies.append(c)
    for c in copies:
        c.wait()


def half_lanes(dz):
    zh = lax.rem(lax.axis_index("zh") + dz, 2)
    return pl.ds(pl.multiple_of(zh * 256, 256), 256)


def lead_products(l_ref, b_s, lanes, m):
    rows = pl.ds(pl.multiple_of(m * 256, 256), 256)
    total = None
    for k in range(8):
        term = nn(l_ref[k, rows, lanes], b_s[k].reshape(256, 1024))
        total = term if total is None else total + term
    return rows, total


def row_products(a_in, b_s, lanes):
    total = None
    for ref, (dx, dz) in zip(a_in, ORDER):
        term = nn(ref[:, lanes], b_s[place(dx, dz)].reshape(256, 1024))
        total = term if total is None else total + term
    return total


def first_kernel(*refs):
    a_in, l_ref, b_ref = refs[:8], refs[8], refs[9]
    own, other, rl, lc_own, lc_other, b_s, sems = refs[10:]
    lanes = half_lanes(0)

    @pl.when(pl.program_id(0) == 0)
    def _():
        fetch(b_ref, b_s, sems)

        def step(m, _):
            rows, total = lead_products(l_ref, b_s, lanes, m)
            lc_own[rows, :] = total[:, :512]
            lc_other[rows, :] = total[:, 512:]
            return 0

        lax.fori_loop(0, 2, step, 0)

    tile = row_products(a_in, b_s, lanes)
    own[...] = tile[:, :512]
    other[...] = tile[:, 512:]
    side = None
    for ref, (dx, dz) in zip(a_in, ORDER):
        term = nt(ref[...], l_ref[place(dx, dz)])
        side = term if side is None else side + term
    rl[...] = side


def second_kernel(*refs):
    a_in, l_ref, b_ref = refs[:8], refs[8], refs[9]
    own0, other0, lc_own0, lc_other0 = refs[10:14]
    own, other, lc_own, lc_other, b_s, sems = refs[15:]
    lanes = half_lanes(1)

    @pl.when(pl.program_id(0) == 0)
    def _():
        fetch(b_ref, b_s, sems)

        def step(m, _):
            rows, total = lead_products(l_ref, b_s, lanes, m)
            lc_own[rows, :] = lc_own0[rows, :] + total[:, :512]
            lc_other[rows, :] = lc_other0[rows, :] + total[:, 512:]
            return 0

        lax.fori_loop(0, 2, step, 0)

    tile = row_products(a_in, b_s, lanes)
    own[...] = own0[...] + tile[:, :512]
    other[...] = other0[...] + tile[:, 512:]


def once(*shape):
    return pl.BlockSpec(shape, lambda m: (0,) * len(shape))


BLOCK = pl.BlockSpec((256, 512), lambda m: (m, 0))
SCRATCH = [pltpu.VMEM((8, 4, 64, 1024), BF), pltpu.SemaphoreType.DMA((4,))]


def gram_first(a, lead, b):
    return pl.pallas_call(
        first_kernel,
        grid=(4,),
        in_specs=[BLOCK] * 8 + [once(8, 512, 512), ANY],
        out_specs=[BLOCK] * 3 + [once(512, 512)] * 2,
        out_shape=[TALL] * 3 + [SQUARE] * 2,
        scratch_shapes=SCRATCH,
        compiler_params=params(40),
        cost_estimate=cost(17),
        name="gram_first",
    )(*a, lead, b)


def gram_second(a, lead, b, own, other, lc_own, lc_other, after):
    return pl.pallas_call(
        second_kernel,
        grid=(4,),
        in_specs=[BLOCK] * 8
        + [once(8, 512, 512), ANY]
        + [BLOCK] * 2
        + [once(512, 512)] * 2
        + [ANY],
        out_specs=[BLOCK] * 2 + [once(512, 512)] * 2,
        out_shape=[TALL] * 2 + [SQUARE] * 2,
        scratch_shapes=SCRATCH,
        compiler_params=params(40),
        cost_estimate=cost(10),
        name="gram_second",
    )(*a, lead, b, own, other, lc_own, lc_other, after)


def column_of(lane):
    k = lax.axis_index("x") * 2 + lax.axis_index("zl")
    return (lane // 256) * 4096 + k * 512 + lax.axis_index("core") * 256 + lane % 256


def row_of(step):
    r = lax.axis_index("y") * 2 + lax.axis_index("zh")
    local = lax.broadcasted_iota(jnp.int32, (256, 512), 0) + step * 256
    return (local // 64) * 512 + r * 64 + local % 64


def panel_kernel(rm, rr, inv_ref, sl_ref, p_ref):
    lane = lax.broadcasted_iota(jnp.int32, (256, 512), 1)
    c = (rm[...] + rr[...]) * F32(1.0 / VARS) + jnp.where(
        row_of(pl.program_id(0)) == lane, sl_ref[...], 0.0
    )
    p_ref[...] = nt(c, inv_ref[...], HI)


def panel(rm, rr, inv, sl):
    return pl.pallas_call(
        panel_kernel,
        grid=(4,),
        in_specs=[BLOCK] * 2 + [once(512, 512), once(1, 512)],
        out_specs=BLOCK,
        out_shape=TALL,
        compiler_params=params(24),
        cost_estimate=cost(5),
        name="panel",
    )(rm, rr, inv, sl)


def final_kernel(tm, tr, p_ref, lm, lr, inv_ref, sc_ref, out_ref, u_ref):
    k = lax.axis_index("x") * 2 + lax.axis_index("zl")
    core = lax.axis_index("core")
    scale = F32(1.0 / VARS)

    @pl.when(pl.program_id(0) == 0)
    def _():
        row = lax.broadcasted_iota(jnp.int32, (512, 512), 0)
        col = column_of(lax.broadcasted_iota(jnp.int32, (512, 512), 1))
        c = (lm[...] + lr[...]) * scale + jnp.where(row == col, sc_ref[...], 0.0)
        u_ref[...] = nn(inv_ref[...], c, HI)

    p = p_ref[...]
    col = column_of(lax.broadcasted_iota(jnp.int32, (256, 512), 1))
    c = (tm[...] + tr[...]) * scale + jnp.where(
        row_of(pl.program_id(0)) == col, sc_ref[...], 0.0
    )
    out_ref[...] = c - nn(p, u_ref[...], HI)

    @pl.when(k == 0)
    def _():
        out_ref[:, :256] = jnp.where(core == 0, p[:, :256], p[:, 256:])


def final(tm, tr, p, lm, lr, inv, sc):
    return pl.pallas_call(
        final_kernel,
        grid=(4,),
        in_specs=[BLOCK] * 3 + [once(512, 512)] * 3 + [once(1, 512)],
        out_specs=BLOCK,
        out_shape=TALL,
        scratch_shapes=[pltpu.VMEM((512, 512), F32)],
        compiler_params=params(32),
        cost_estimate=cost(9),
        name="final",
    )(tm, tr, p, lm, lr, inv, sc)


def shift(v, axis, by):
    n = lax.axis_size(axis)
    return lax.ppermute(v, axis, [(i, (i + by) % n) for i in range(n)])


def after(v, *others):
    return lax.optimization_barrier((v, *others))[0]


def near(v, axis):
    return shift(v, axis, -1), shift(v, axis, 1)


def body(samples, shrink):
    k = lax.axis_index("x") * 2 + lax.axis_index("zl")
    core = lax.axis_index("core")
    zz = ("zh", "zl")
    rows, up, down, lead, strip = prep(samples)
    cols = lax.all_to_all(strip, ("x", "zl"), split_axis=0, concat_axis=0, tiled=True)

    lead_z = shift(lead, "zl", 1)
    rows_z = jnp.concatenate([shift(up, zz, 1), shift(down, zz, -1)], axis=0)
    l_up, l_down = near(lead, "x")
    lead_z, l_up, l_down, cols = lax.optimization_barrier((lead_z, l_up, l_down, cols))
    lz_up, lz_down = near(lead_z, "x")
    l_far, lz_far = shift(l_down, "x", 1), shift(lz_up, "x", -1)
    cols_z = shift(cols, "zh", 1)
    b_own = lax.all_gather(cols, "y")
    b_z = lax.all_gather(cols_z, "y")
    a_up, a_down = near(rows, "x")
    az_up, az_down = near(rows_z, "x")
    g, lead_all = lead_gram([lead, l_up, l_down, l_far, lead_z, lz_up, lz_down, lz_far])
    sl = shrink[:PANEL].reshape(1, PANEL)
    half_a, half_inv = chol_half(g, shift(g, "core", 1), sl)
    inv = chol_rest(half_a, half_inv)
    a_far, az_far = shift(a_down, "x", 1), shift(az_up, "x", -1)

    a = [rows, a_up, a_down, a_far, rows_z, az_up, az_down, az_far]
    parts = gram_first(a, lead_all, b_own)
    rl = parts[2]
    p = panel(rl, shift(rl, "core", 1), inv, sl)
    own, other, lc_own, lc_other = gram_second(a, lead_all, b_z, *parts[:2], *parts[3:], p)
    sc = lax.dynamic_slice(shrink.reshape(2, 16, 256), (0, 2 * k + core, 0), (2, 1, 256))
    sc = sc.reshape(1, 512)
    out = final(own, shift(other, "core", 1), p, lc_own, shift(lc_other, "core", 1), inv, sc)
    return out.reshape(1, 1024, 1, 512)


def solution(mesh):
    fine = Mesh(mesh.devices.reshape(4, 2, 4, 2, 2), ("y", "zh", "x", "zl", "core"))
    return jax.shard_map(
        body,
        mesh=fine,
        in_specs=(P(("x", "zl", "core"), None), P()),
        out_specs=P(("y", "zh"), None, ("x", "zl", "core"), None),
        check_vma=False,
    )
```

```python
import jax
import jax.numpy as jnp
from jax import lax
from jax.experimental import pallas as pl
from jax.experimental.pallas import tpu as pltpu
from jax.sharding import Mesh, PartitionSpec as P

PANEL = 512
VARS = 8192
ROWS = 512
HI = lax.Precision.HIGHEST
F32 = jnp.float32
BF = jnp.bfloat16
MB = 1 << 20


def cost(us):
    return pl.CostEstimate(flops=us << 30, bytes_accessed=1 << 16, transcendentals=0)


ANY = pl.BlockSpec(memory_space=pl.ANY)
VM = pl.BlockSpec(memory_space=pltpu.VMEM)


def params(mb):
    return pltpu.CompilerParams(vmem_limit_bytes=mb * MB)


def nt(a, b, precision=None):
    return lax.dot_general(
        a, b, (((1,), (1,)), ((), ())), precision=precision, preferred_element_type=F32
    )


def nn(a, b, precision=None):
    return lax.dot_general(
        a, b, (((1,), (0,)), ((), ())), precision=precision, preferred_element_type=F32
    )


def prep_kernel(lo_ref, hi_ref, rows_ref, up_ref, down_ref, lead_ref, strip_ref, pick_ref):
    y, zh, zl = lax.axis_index("y"), lax.axis_index("zh"), lax.axis_index("zl")
    r = y * 2 + zh
    core = lax.axis_index("core")
    @pl.when(pl.program_id(0) == 0)
    def _():
        j = lax.broadcasted_iota(jnp.int32, (512, 128), 0)
        i = lax.broadcasted_iota(jnp.int32, (512, 128), 1)
        for h, by in enumerate((1, 3)):
            other = y * 2 + lax.rem(zh * 2 + zl + by, 4) // 2
            want = jnp.where(i < 64, r * 64 + i, other * 64 + i - 64)
            pick_ref[h] = jnp.where(j == want, 1.0, 0.0).astype(BF)

    mine = pl.ds(pl.multiple_of((zh * 4 + y) * 64, 64), 64)
    for h, (ref, out) in enumerate(((lo_ref, up_ref), (hi_ref, down_ref))):
        picked = nn(ref[...], pick_ref[h]).astype(BF).T
        rows_ref[h, 0] = picked[:64]
        out[0] = picked[64:]
        part = ref[mine, :]
        left, right = part[:, :256], part[:, 256:]
        strip_ref[0, :, h * 256 : h * 256 + 256] = jnp.where(core == 0, left, right)
        strip_ref[0, :, 512 + h * 256 : 768 + h * 256] = jnp.where(core == 0, right, left)

    @pl.when(pl.program_id(0) == 0)
    def _():
        lead_ref[...] = lo_ref[...].T


def prep(x):
    rows, up, down, lead, strip = pl.pallas_call(
        prep_kernel,
        grid=(8,),
        in_specs=[
            pl.BlockSpec((ROWS, 512), lambda k: (0, k)),
            pl.BlockSpec((ROWS, 512), lambda k: (0, k + 8)),
        ],
        out_specs=[
            pl.BlockSpec((2, 1, 64, ROWS), lambda k: (0, k, 0, 0)),
            pl.BlockSpec((1, 64, ROWS), lambda k: (k, 0, 0)),
            pl.BlockSpec((1, 64, ROWS), lambda k: (k, 0, 0)),
            pl.BlockSpec((512, ROWS), lambda k: (0, 0)),
            pl.BlockSpec((1, 64, 1024), lambda k: (k, 0, 0)),
        ],
        out_shape=[
            jax.ShapeDtypeStruct((2, 8, 64, ROWS), BF),
            jax.ShapeDtypeStruct((8, 64, ROWS), BF),
            jax.ShapeDtypeStruct((8, 64, ROWS), BF),
            jax.ShapeDtypeStruct((512, ROWS), BF),
            jax.ShapeDtypeStruct((8, 64, 1024), BF),
        ],
        scratch_shapes=[pltpu.VMEM((2, 512, 128), BF)],
        compiler_params=params(58),
        cost_estimate=cost(9),
        name="prep",
    )(x, x)
    return rows.reshape(1024, ROWS), up.reshape(512, ROWS), down.reshape(512, ROWS), lead, strip


def place(dx, dz):
    return lax.rem(lax.axis_index("x") + dx, 4) * 2 + lax.rem(lax.axis_index("zl") + dz, 2)


def lead_kernel(*refs):
    gram_ref, all_ref = refs[-2:]
    for dz in range(2):
        for n, dx in enumerate((0, 1, 3, 2)):
            all_ref[place(dx, dz)] = refs[4 * dz + n][...]
    total = None
    for k in range(8):
        v = all_ref[k]
        term = nt(v, v)
        total = term if total is None else total + term
    gram_ref[...] = total


def lead_gram(pieces):
    return pl.pallas_call(
        lead_kernel,
        in_specs=[VM] * len(pieces),
        out_specs=[VM, VM],
        out_shape=[
            jax.ShapeDtypeStruct((512, 512), F32),
            jax.ShapeDtypeStruct((8, 512, 512), BF),
        ],
        compiler_params=params(24),
        cost_estimate=cost(4),
        name="lead_gram",
    )(*pieces)


def factor128(block):
    tiles = [block[8 * t : 8 * t + 8, :] for t in range(16)]
    lane = lax.broadcasted_iota(jnp.int32, (8, 128), 1)
    sub = lax.broadcasted_iota(jnp.int32, (8, 128), 0)
    out = []
    for g in range(16):
        j0 = 8 * g
        group = (lane >= j0) & (lane < j0 + 8)
        cols = [jnp.broadcast_to(tiles[g][:, j0 + s : j0 + s + 1], (8, 128)) for s in range(8)]
        jordan = jnp.where(group, jnp.where(lane - j0 == sub, 1.0, 0.0), tiles[g])
        kept = jnp.zeros((8, 128), F32)
        invs = jnp.ones((8, 128), F32)
        for s in range(8):
            here = sub == s
            inv = 1.0 / jnp.broadcast_to(cols[s][s : s + 1, :], (8, 128))
            row = jnp.broadcast_to(jordan[s : s + 1, :], (8, 128))
            kept = jnp.where(here, row, kept)
            invs = jnp.where(here, inv, invs)
            factor = jnp.where(here, 1.0 - inv, cols[s] * inv)
            jordan = jordan - factor * row
            for q in range(s + 1, 8):
                cols[q] = cols[q] - factor * jnp.broadcast_to(cols[q][s : s + 1, :], (8, 128))
        out.append(jnp.where(lane <= sub + j0, kept * jnp.sqrt(invs), 0.0))
        for t in range(g + 1, 16):
            tile = jnp.where(group, 0.0, tiles[t])
            for s in range(8):
                tile = tile - tiles[t][:, j0 + s : j0 + s + 1] * jordan[s : s + 1, :]
            tiles[t] = tile
    return jnp.concatenate(out, axis=0)


def chol_blocks(a_ref, inv_ref, blocks):
    for b in blocks:
        lo, hi = b * 128, b * 128 + 128
        w = factor128(a_ref[lo:hi, lo:hi])
        if b > 0:
            mid = nn(a_ref[lo:hi, :lo], inv_ref[:lo, :lo], HI)
            inv_ref[lo:hi, :lo] = -nn(w, mid, HI)
        inv_ref[lo:hi, lo:hi] = w
        if b < 3:
            below = nt(a_ref[hi:, lo:hi], w, HI)
            a_ref[hi:, lo:hi] = below
            a_ref[hi:, hi:] = a_ref[hi:, hi:] - nt(below, below, HI)


def chol_first(g0, g1, shrink_ref, a_ref, inv_ref):
    i = lax.broadcasted_iota(jnp.int32, (512, 512), 0)
    j = lax.broadcasted_iota(jnp.int32, (512, 512), 1)
    a_ref[...] = (g0[...] + g1[...]) * F32(1.0 / VARS) + jnp.where(
        i == j, shrink_ref[...], 0.0
    )
    inv_ref[...] = jnp.zeros((512, 512), F32)
    chol_blocks(a_ref, inv_ref, (0, 1))


def chol_second(a0, i0, inv_ref, a_ref):
    a_ref[...] = a0[...]
    inv_ref[...] = i0[...]
    chol_blocks(a_ref, inv_ref, (2, 3))


SQUARE = jax.ShapeDtypeStruct((512, 512), F32)


def chol_half(g0, g1, shrink_lead):
    return pl.pallas_call(
        chol_first,
        in_specs=[VM] * 3,
        out_specs=[VM, VM],
        out_shape=[SQUARE, SQUARE],
        compiler_params=params(16),
        cost_estimate=cost(80),
        name="chol_first",
    )(g0, g1, shrink_lead)


def chol_rest(a, inv):
    return pl.pallas_call(
        chol_second,
        in_specs=[VM, VM],
        out_specs=VM,
        out_shape=SQUARE,
        scratch_shapes=[pltpu.VMEM((512, 512), F32)],
        compiler_params=params(16),
        cost_estimate=cost(80),
        name="chol_second",
    )(a, inv)


TALL = jax.ShapeDtypeStruct((1024, 512), F32)
NEAR = tuple((dx, dz) for dz in range(2) for dx in (0, 1, 3))
FAR = ((2, 0), (2, 1))


def fetch(b_ref, b_s, sems):
    copies = []
    for y in range(4):
        c = pltpu.make_async_copy(b_ref.at[y], b_s.at[:, y], sems.at[y])
        c.start()
        copies.append(c)
    for c in copies:
        c.wait()


def half_lanes(dz):
    zh = lax.rem(lax.axis_index("zh") + dz, 2)
    return pl.ds(pl.multiple_of(zh * 256, 256), 256)


def lead_products(l_ref, b_s, lanes, m):
    rows = pl.ds(pl.multiple_of(m * 256, 256), 256)
    total = None
    for k in range(8):
        term = nn(l_ref[k, rows, lanes], b_s[k].reshape(256, 1024))
        total = term if total is None else total + term
    return rows, total


def row_products(a_in, order, b_s, lanes):
    total = None
    for ref, (dx, dz) in zip(a_in, order):
        term = nn(ref[:, lanes], b_s[place(dx, dz)].reshape(256, 1024))
        total = term if total is None else total + term
    return total


def side_products(a_in, order, l_ref):
    total = None
    for ref, (dx, dz) in zip(a_in, order):
        term = nt(ref[...], l_ref[place(dx, dz)])
        total = term if total is None else total + term
    return total


def first_kernel(*refs):
    a_in, l_ref, b_ref = refs[:6], refs[6], refs[7]
    own, other, rl, lc_own, lc_other, far_ref, b_s, sems = refs[9:]
    lanes = half_lanes(0)

    @pl.when(pl.program_id(0) == 0)
    def _():
        fetch(b_ref, b_s, sems)

        def step(m, _):
            rows, total = lead_products(l_ref, b_s, lanes, m)
            lc_own[rows, :] = total[:, :512]
            lc_other[rows, :] = total[:, 512:]
            return 0

        lax.fori_loop(0, 2, step, 0)
        for dz in range(2):
            far_ref[dz] = b_s[place(2, dz)].reshape(256, 1024)

    tile = row_products(a_in, NEAR, b_s, lanes)
    own[...] = tile[:, :512]
    other[...] = tile[:, 512:]
    rl[...] = side_products(a_in, NEAR, l_ref)


def middle_kernel(a0, a1, l_ref, far_ref, own0, other0, rl0, own, other, rl):
    lanes = half_lanes(0)
    tile = nn(a0[:, lanes], far_ref[0]) + nn(a1[:, lanes], far_ref[1])
    own[...] = own0[...] + tile[:, :512]
    other[...] = other0[...] + tile[:, 512:]
    rl[...] = rl0[...] + side_products((a0, a1), FAR, l_ref)


def second_kernel(*refs):
    a_in, l_ref, b_ref = refs[:8], refs[8], refs[9]
    own0, other0, lc_own0, lc_other0 = refs[10:14]
    own, other, lc_own, lc_other, b_s, sems = refs[14:]
    lanes = half_lanes(1)

    @pl.when(pl.program_id(0) == 0)
    def _():
        fetch(b_ref, b_s, sems)

        def step(m, _):
            rows, total = lead_products(l_ref, b_s, lanes, m)
            lc_own[rows, :] = lc_own0[rows, :] + total[:, :512]
            lc_other[rows, :] = lc_other0[rows, :] + total[:, 512:]
            return 0

        lax.fori_loop(0, 2, step, 0)

    tile = row_products(a_in, NEAR + FAR, b_s, lanes)
    own[...] = own0[...] + tile[:, :512]
    other[...] = other0[...] + tile[:, 512:]


def once(*shape):
    return pl.BlockSpec(shape, lambda m: (0,) * len(shape))


BLOCK = pl.BlockSpec((256, 512), lambda m: (m, 0))
SCRATCH = [pltpu.VMEM((8, 4, 64, 1024), BF), pltpu.SemaphoreType.DMA((4,))]


def gram_first(a, lead, b, after):
    return pl.pallas_call(
        first_kernel,
        grid=(4,),
        in_specs=[BLOCK] * 6 + [once(8, 512, 512), ANY, ANY],
        out_specs=[BLOCK] * 3 + [once(512, 512)] * 2 + [once(2, 256, 1024)],
        out_shape=[TALL] * 3 + [SQUARE] * 2 + [jax.ShapeDtypeStruct((2, 256, 1024), BF)],
        scratch_shapes=SCRATCH,
        compiler_params=params(40),
        cost_estimate=cost(17),
        name="gram_first",
    )(*a, lead, b, after)


def gram_middle(a, lead, far, own, other, rl):
    return pl.pallas_call(
        middle_kernel,
        grid=(4,),
        in_specs=[BLOCK] * 2 + [once(8, 512, 512), once(2, 256, 1024)] + [BLOCK] * 3,
        out_specs=[BLOCK] * 3,
        out_shape=[TALL] * 3,
        compiler_params=params(40),
        cost_estimate=cost(5),
        name="gram_middle",
    )(*a, lead, far, own, other, rl)


def gram_second(a, lead, b, own, other, lc_own, lc_other):
    return pl.pallas_call(
        second_kernel,
        grid=(4,),
        in_specs=[BLOCK] * 8
        + [once(8, 512, 512), ANY]
        + [BLOCK] * 2
        + [once(512, 512)] * 2,
        out_specs=[BLOCK] * 2 + [once(512, 512)] * 2,
        out_shape=[TALL] * 2 + [SQUARE] * 2,
        scratch_shapes=SCRATCH,
        compiler_params=params(40),
        cost_estimate=cost(10),
        name="gram_second",
    )(*a, lead, b, own, other, lc_own, lc_other)


def column_of(lane):
    k = lax.axis_index("x") * 2 + lax.axis_index("zl")
    return (lane // 256) * 4096 + k * 512 + lax.axis_index("core") * 256 + lane % 256


def row_of(step):
    r = lax.axis_index("y") * 2 + lax.axis_index("zh")
    local = lax.broadcasted_iota(jnp.int32, (256, 512), 0) + step * 256
    return (local // 64) * 512 + r * 64 + local % 64


def panel_kernel(rm, rr, inv_ref, sl_ref, p_ref):
    lane = lax.broadcasted_iota(jnp.int32, (256, 512), 1)
    c = (rm[...] + rr[...]) * F32(1.0 / VARS) + jnp.where(
        row_of(pl.program_id(0)) == lane, sl_ref[...], 0.0
    )
    p_ref[...] = nt(c, inv_ref[...], HI)


def panel(rm, rr, inv, sl):
    return pl.pallas_call(
        panel_kernel,
        grid=(4,),
        in_specs=[BLOCK] * 2 + [once(512, 512), once(1, 512)],
        out_specs=BLOCK,
        out_shape=TALL,
        compiler_params=params(24),
        cost_estimate=cost(5),
        name="panel",
    )(rm, rr, inv, sl)


def final_kernel(tm, tr, p_ref, lm, lr, inv_ref, sc_ref, out_ref, u_ref):
    k = lax.axis_index("x") * 2 + lax.axis_index("zl")
    core = lax.axis_index("core")
    scale = F32(1.0 / VARS)

    @pl.when(pl.program_id(0) == 0)
    def _():
        row = lax.broadcasted_iota(jnp.int32, (512, 512), 0)
        col = column_of(lax.broadcasted_iota(jnp.int32, (512, 512), 1))
        c = (lm[...] + lr[...]) * scale + jnp.where(row == col, sc_ref[...], 0.0)
        u_ref[...] = nn(inv_ref[...], c, HI)

    p = p_ref[...]
    col = column_of(lax.broadcasted_iota(jnp.int32, (256, 512), 1))
    c = (tm[...] + tr[...]) * scale + jnp.where(
        row_of(pl.program_id(0)) == col, sc_ref[...], 0.0
    )
    out_ref[:, 0, :] = c - nn(p, u_ref[...], HI)

    @pl.when(k == 0)
    def _():
        out_ref[:, 0, :256] = jnp.where(core == 0, p[:, :256], p[:, 256:])


def final(tm, tr, p, lm, lr, inv, sc):
    return pl.pallas_call(
        final_kernel,
        grid=(4,),
        in_specs=[BLOCK] * 3 + [once(512, 512)] * 3 + [once(1, 512)],
        out_specs=pl.BlockSpec((256, 1, 512), lambda m: (m, 0, 0)),
        out_shape=jax.ShapeDtypeStruct((1024, 1, 512), F32),
        scratch_shapes=[pltpu.VMEM((512, 512), F32)],
        compiler_params=params(32),
        cost_estimate=cost(9),
        name="final",
    )(tm, tr, p, lm, lr, inv, sc)


def shift(v, axis, by):
    n = lax.axis_size(axis)
    return lax.ppermute(v, axis, [(i, (i + by) % n) for i in range(n)])


def after(v, *others):
    return lax.optimization_barrier((v, *others))[0]


def near(v, axis):
    return shift(v, axis, -1), shift(v, axis, 1)


def body(samples, shrink):
    k = lax.axis_index("x") * 2 + lax.axis_index("zl")
    core = lax.axis_index("core")
    zz = ("zh", "zl")
    rows, up, down, lead, strip = prep(samples)
    cols = lax.all_to_all(strip, ("x", "zl"), split_axis=0, concat_axis=0, tiled=True)

    lead_z = shift(lead, "zl", 1)
    rows_z = jnp.concatenate([shift(up, zz, 1), shift(down, zz, -1)], axis=0)
    l_up, l_down = near(lead, "x")
    lead_z, l_up, l_down, cols = lax.optimization_barrier((lead_z, l_up, l_down, cols))
    lz_up, lz_down = near(lead_z, "x")
    l_far, lz_far = shift(l_down, "x", 1), shift(lz_up, "x", -1)
    cols_z = shift(cols, "zh", 1)
    b_own = lax.all_gather(cols, "y")
    b_z = lax.all_gather(cols_z, "y")
    rows = after(rows, lead_z)
    a_up, a_down = near(rows, "x")
    az_up, az_down = near(rows_z, "x")
    g, lead_all = lead_gram([lead, l_up, l_down, l_far, lead_z, lz_up, lz_down, lz_far])
    sl = shrink[:PANEL].reshape(1, PANEL)
    half_a, half_inv = chol_half(g, shift(g, "core", 1), sl)
    inv = chol_rest(half_a, half_inv)
    a_far, az_far = shift(a_down, "x", 1), shift(az_up, "x", -1)

    a = [rows, a_up, a_down, rows_z, az_up, az_down]
    own, other, rl, lc_own, lc_other, b_part = gram_first(a, lead_all, b_own, inv)
    own, other, rl = gram_middle([a_far, az_far], lead_all, b_part, own, other, rl)
    p = panel(rl, shift(rl, "core", 1), inv, sl)
    a = [*a, a_far, az_far]
    own, other, lc_own, lc_other = gram_second(a, lead_all, b_z, own, other, lc_own, lc_other)
    sc = lax.dynamic_slice(shrink.reshape(2, 16, 256), (0, 2 * k + core, 0), (2, 1, 256))
    sc = sc.reshape(1, 512)
    out = final(own, shift(other, "core", 1), p, lc_own, shift(lc_other, "core", 1), inv, sc)
    return out.reshape(1, 1024, 1, 512)


def solution(mesh):
    fine = Mesh(mesh.devices.reshape(4, 2, 4, 2, 2), ("y", "zh", "x", "zl", "core"))
    return jax.shard_map(
        body,
        mesh=fine,
        in_specs=(P(("x", "zl", "core"), None), P()),
        out_specs=P(("y", "zh"), None, ("x", "zl", "core"), None),
        check_vma=False,
    )
```

```python
import jax
import jax.numpy as jnp
from jax import lax
from jax.experimental import pallas as pl
from jax.experimental.pallas import tpu as pltpu
from jax.sharding import Mesh, PartitionSpec as P

PANEL = 512
VARS = 8192
ROWS = 512
HI = lax.Precision.HIGHEST
F32 = jnp.float32
BF = jnp.bfloat16
MB = 1 << 20


def cost(us):
    return pl.CostEstimate(flops=us << 30, bytes_accessed=1 << 16, transcendentals=0)


ANY = pl.BlockSpec(memory_space=pl.ANY)
VM = pl.BlockSpec(memory_space=pltpu.VMEM)


def params(mb):
    return pltpu.CompilerParams(vmem_limit_bytes=mb * MB)


def nt(a, b, precision=None):
    return lax.dot_general(
        a, b, (((1,), (1,)), ((), ())), precision=precision, preferred_element_type=F32
    )


def nn(a, b, precision=None):
    return lax.dot_general(
        a, b, (((1,), (0,)), ((), ())), precision=precision, preferred_element_type=F32
    )


def prep_kernel(lo_ref, hi_ref, rows_ref, up_ref, down_ref, lead_ref, strip_ref, pick_ref):
    y, zh, zl = lax.axis_index("y"), lax.axis_index("zh"), lax.axis_index("zl")
    r = y * 2 + zh
    core = lax.axis_index("core")
    @pl.when(pl.program_id(0) == 0)
    def _():
        j = lax.broadcasted_iota(jnp.int32, (512, 128), 0)
        i = lax.broadcasted_iota(jnp.int32, (512, 128), 1)
        for h, by in enumerate((1, 3)):
            other = y * 2 + lax.rem(zh * 2 + zl + by, 4) // 2
            want = jnp.where(i < 64, r * 64 + i, other * 64 + i - 64)
            pick_ref[h] = jnp.where(j == want, 1.0, 0.0).astype(BF)

    mine = pl.ds(pl.multiple_of((zh * 4 + y) * 64, 64), 64)
    for h, (ref, out) in enumerate(((lo_ref, up_ref), (hi_ref, down_ref))):
        picked = nn(ref[...], pick_ref[h]).astype(BF).T
        rows_ref[h, 0] = picked[:64]
        out[0] = picked[64:]
        part = ref[mine, :]
        left, right = part[:, :256], part[:, 256:]
        strip_ref[0, :, h * 256 : h * 256 + 256] = jnp.where(core == 0, left, right)
        strip_ref[0, :, 512 + h * 256 : 768 + h * 256] = jnp.where(core == 0, right, left)

    @pl.when(pl.program_id(0) == 0)
    def _():
        lead_ref[...] = lo_ref[...].T


def prep(x):
    rows, up, down, lead, strip = pl.pallas_call(
        prep_kernel,
        grid=(8,),
        in_specs=[
            pl.BlockSpec((ROWS, 512), lambda k: (0, k)),
            pl.BlockSpec((ROWS, 512), lambda k: (0, k + 8)),
        ],
        out_specs=[
            pl.BlockSpec((2, 1, 64, ROWS), lambda k: (0, k, 0, 0)),
            pl.BlockSpec((1, 64, ROWS), lambda k: (k, 0, 0)),
            pl.BlockSpec((1, 64, ROWS), lambda k: (k, 0, 0)),
            pl.BlockSpec((512, ROWS), lambda k: (0, 0)),
            pl.BlockSpec((1, 64, 1024), lambda k: (k, 0, 0)),
        ],
        out_shape=[
            jax.ShapeDtypeStruct((2, 8, 64, ROWS), BF),
            jax.ShapeDtypeStruct((8, 64, ROWS), BF),
            jax.ShapeDtypeStruct((8, 64, ROWS), BF),
            jax.ShapeDtypeStruct((512, ROWS), BF),
            jax.ShapeDtypeStruct((8, 64, 1024), BF),
        ],
        scratch_shapes=[pltpu.VMEM((2, 512, 128), BF)],
        compiler_params=params(58),
        cost_estimate=cost(9),
        name="prep",
    )(x, x)
    return rows.reshape(1024, ROWS), up.reshape(512, ROWS), down.reshape(512, ROWS), lead, strip


def place(dx, dz):
    return lax.rem(lax.axis_index("x") + dx, 4) * 2 + lax.rem(lax.axis_index("zl") + dz, 2)


def lead_kernel(*refs):
    gram_ref, all_ref = refs[-2:]
    for dz in range(2):
        for n, dx in enumerate((0, 1, 3, 2)):
            all_ref[place(dx, dz)] = refs[4 * dz + n][...]
    total = None
    for k in range(8):
        v = all_ref[k]
        term = nt(v, v)
        total = term if total is None else total + term
    gram_ref[...] = total


def lead_gram(pieces):
    return pl.pallas_call(
        lead_kernel,
        in_specs=[VM] * len(pieces),
        out_specs=[VM, VM],
        out_shape=[
            jax.ShapeDtypeStruct((512, 512), F32),
            jax.ShapeDtypeStruct((8, 512, 512), BF),
        ],
        compiler_params=params(24),
        cost_estimate=cost(4),
        name="lead_gram",
    )(*pieces)


def factor128(block):
    tiles = [block[8 * t : 8 * t + 8, :] for t in range(16)]
    lane = lax.broadcasted_iota(jnp.int32, (8, 128), 1)
    sub = lax.broadcasted_iota(jnp.int32, (8, 128), 0)
    out = []
    for g in range(16):
        j0 = 8 * g
        group = (lane >= j0) & (lane < j0 + 8)
        cols = [jnp.broadcast_to(tiles[g][:, j0 + s : j0 + s + 1], (8, 128)) for s in range(8)]
        jordan = jnp.where(group, jnp.where(lane - j0 == sub, 1.0, 0.0), tiles[g])
        kept = jnp.zeros((8, 128), F32)
        invs = jnp.ones((8, 128), F32)
        for s in range(8):
            here = sub == s
            inv = 1.0 / jnp.broadcast_to(cols[s][s : s + 1, :], (8, 128))
            row = jnp.broadcast_to(jordan[s : s + 1, :], (8, 128))
            kept = jnp.where(here, row, kept)
            invs = jnp.where(here, inv, invs)
            factor = jnp.where(here, 1.0 - inv, cols[s] * inv)
            jordan = jordan - factor * row
            for q in range(s + 1, 8):
                cols[q] = cols[q] - factor * jnp.broadcast_to(cols[q][s : s + 1, :], (8, 128))
        out.append(jnp.where(lane <= sub + j0, kept * jnp.sqrt(invs), 0.0))
        for t in range(g + 1, 16):
            tile = jnp.where(group, 0.0, tiles[t])
            for s in range(8):
                tile = tile - tiles[t][:, j0 + s : j0 + s + 1] * jordan[s : s + 1, :]
            tiles[t] = tile
    return jnp.concatenate(out, axis=0)


def chol_blocks(a_ref, inv_ref, blocks):
    for b in blocks:
        lo, hi = b * 128, b * 128 + 128
        w = factor128(a_ref[lo:hi, lo:hi])
        if b > 0:
            mid = nn(a_ref[lo:hi, :lo], inv_ref[:lo, :lo], HI)
            inv_ref[lo:hi, :lo] = -nn(w, mid, HI)
        inv_ref[lo:hi, lo:hi] = w
        if b < 3:
            below = nt(a_ref[hi:, lo:hi], w, HI)
            a_ref[hi:, lo:hi] = below
            a_ref[hi:, hi:] = a_ref[hi:, hi:] - nt(below, below, HI)


def chol_first(g0, g1, shrink_ref, a_ref, inv_ref):
    i = lax.broadcasted_iota(jnp.int32, (512, 512), 0)
    j = lax.broadcasted_iota(jnp.int32, (512, 512), 1)
    a_ref[...] = (g0[...] + g1[...]) * F32(1.0 / VARS) + jnp.where(
        i == j, shrink_ref[...], 0.0
    )
    inv_ref[...] = jnp.zeros((512, 512), F32)
    chol_blocks(a_ref, inv_ref, (0, 1))


def chol_second(a0, i0, inv_ref, a_ref):
    a_ref[...] = a0[...]
    inv_ref[...] = i0[...]
    chol_blocks(a_ref, inv_ref, (2, 3))


SQUARE = jax.ShapeDtypeStruct((512, 512), F32)


def chol_half(g0, g1, shrink_lead):
    return pl.pallas_call(
        chol_first,
        in_specs=[VM] * 3,
        out_specs=[VM, VM],
        out_shape=[SQUARE, SQUARE],
        compiler_params=params(16),
        cost_estimate=cost(80),
        name="chol_first",
    )(g0, g1, shrink_lead)


def chol_rest(a, inv):
    return pl.pallas_call(
        chol_second,
        in_specs=[VM, VM],
        out_specs=VM,
        out_shape=SQUARE,
        scratch_shapes=[pltpu.VMEM((512, 512), F32)],
        compiler_params=params(16),
        cost_estimate=cost(80),
        name="chol_second",
    )(a, inv)


TALL = jax.ShapeDtypeStruct((1024, 512), F32)
NEAR = tuple((dx, dz) for dz in range(2) for dx in (0, 1, 3))
FAR = ((2, 0), (2, 1))


def fetch(b_ref, b_s, sems):
    copies = []
    for y in range(4):
        c = pltpu.make_async_copy(b_ref.at[y], b_s.at[:, y], sems.at[y])
        c.start()
        copies.append(c)
    for c in copies:
        c.wait()


def other_zh():
    return lax.rem(lax.axis_index("zh") + 1, 2)


def half_lanes(dz):
    zh = lax.rem(lax.axis_index("zh") + dz, 2)
    return pl.ds(pl.multiple_of(zh * 256, 256), 256)


def lead_products(l_ref, b_s, lanes, m):
    rows = pl.ds(pl.multiple_of(m * 256, 256), 256)
    total = None
    for k in range(8):
        term = nn(l_ref[k, rows, lanes], b_s[k].reshape(256, 1024))
        total = term if total is None else total + term
    return rows, total


def row_products(a_in, order, b_s, lanes):
    total = None
    for ref, (dx, dz) in zip(a_in, order):
        term = nn(ref[:, lanes], b_s[place(dx, dz)].reshape(256, 1024))
        total = term if total is None else total + term
    return total


def side_products(a_in, order, l_ref):
    total = None
    for ref, (dx, dz) in zip(a_in, order):
        term = nt(ref[...], l_ref[place(dx, dz)])
        total = term if total is None else total + term
    return total


def first_kernel(*refs):
    a_in, l_ref, b_ref = refs[:6], refs[6], refs[7]
    own, other, rl, lc_own, lc_other, far_ref, b_s, sems = refs[9:]
    lanes = half_lanes(0)

    @pl.when(pl.program_id(0) == 0)
    def _():
        fetch(b_ref, b_s, sems)

        def step(m, _):
            rows, total = lead_products(l_ref, b_s, lanes, m)
            lc_own[rows, :] = total[:, :512]
            lc_other[rows, :] = total[:, 512:]
            return 0

        lax.fori_loop(0, 2, step, 0)
        for dz in range(2):
            far_ref[dz] = b_s[place(2, dz)].reshape(256, 1024)

    tile = row_products(a_in, NEAR, b_s, lanes)
    own[...] = tile[:, :512]
    other[...] = tile[:, 512:]
    rl[...] = side_products(a_in, NEAR, l_ref)


def middle_kernel(a0, a1, l_ref, rl0, rl):
    rl[...] = rl0[...] + side_products((a0, a1), FAR, l_ref)


def second_kernel(*refs):
    near_in, far_in, l_ref, b_ref, far_ref = refs[:6], refs[6:8], refs[8], refs[9], refs[10]
    own0, other0, lc_own0, lc_other0 = refs[11:15]
    own, other, lc_own, lc_other, b_s, sems = refs[15:]
    half = slice(None)

    @pl.when(pl.program_id(0) == 0)
    def _():
        fetch(b_ref, b_s, sems)

        def step(m, _):
            rows, total = lead_products(l_ref, b_s, half, m)
            lc_own[rows, :] = lc_own0[rows, :] + total[:, :512]
            lc_other[rows, :] = lc_other0[rows, :] + total[:, 512:]
            return 0

        lax.fori_loop(0, 2, step, 0)

    tile = row_products(near_in, NEAR, b_s, half)
    tile = tile + row_products(far_in, FAR, b_s, half_lanes(1))
    for dz in range(2):
        tile = tile + nn(far_in[dz][:, half_lanes(0)], far_ref[dz])
    own[...] = own0[...] + tile[:, :512]
    other[...] = other0[...] + tile[:, 512:]


def once(*shape):
    return pl.BlockSpec(shape, lambda m: (0,) * len(shape))


BLOCK = pl.BlockSpec((256, 512), lambda m: (m, 0))
SCRATCH = [pltpu.VMEM((8, 4, 64, 1024), BF), pltpu.SemaphoreType.DMA((4,))]


def gram_first(a, lead, b, after):
    return pl.pallas_call(
        first_kernel,
        grid=(4,),
        in_specs=[BLOCK] * 6 + [once(8, 512, 512), ANY, ANY],
        out_specs=[BLOCK] * 3 + [once(512, 512)] * 2 + [once(2, 256, 1024)],
        out_shape=[TALL] * 3 + [SQUARE] * 2 + [jax.ShapeDtypeStruct((2, 256, 1024), BF)],
        scratch_shapes=SCRATCH,
        compiler_params=params(40),
        cost_estimate=cost(17),
        name="gram_first",
    )(*a, lead, b, after)


def gram_middle(a, lead, rl):
    return pl.pallas_call(
        middle_kernel,
        grid=(4,),
        in_specs=[BLOCK] * 2 + [once(8, 512, 512)] + [BLOCK],
        out_specs=BLOCK,
        out_shape=TALL,
        compiler_params=params(40),
        cost_estimate=cost(5),
        name="gram_middle",
    )(*a, lead, rl)


def gram_second(near_a, far_a, lead, b, b_part, own, other, lc_own, lc_other):
    return pl.pallas_call(
        second_kernel,
        grid=(4,),
        in_specs=[pl.BlockSpec((256, 256), lambda m: (m, other_zh()))] * 6
        + [BLOCK] * 2
        + [pl.BlockSpec((8, 512, 256), lambda m: (0, 0, other_zh())), ANY, once(2, 256, 1024)]
        + [BLOCK] * 2
        + [once(512, 512)] * 2,
        out_specs=[BLOCK] * 2 + [once(512, 512)] * 2,
        out_shape=[TALL] * 2 + [SQUARE] * 2,
        scratch_shapes=SCRATCH,
        compiler_params=params(40),
        cost_estimate=cost(10),
        name="gram_second",
    )(*near_a, *far_a, lead, b, b_part, own, other, lc_own, lc_other)


def column_of(lane):
    k = lax.axis_index("x") * 2 + lax.axis_index("zl")
    return (lane // 256) * 4096 + k * 512 + lax.axis_index("core") * 256 + lane % 256


def row_of(step):
    r = lax.axis_index("y") * 2 + lax.axis_index("zh")
    local = lax.broadcasted_iota(jnp.int32, (256, 512), 0) + step * 256
    return (local // 64) * 512 + r * 64 + local % 64


def panel_kernel(rm, rr, inv_ref, sl_ref, p_ref):
    lane = lax.broadcasted_iota(jnp.int32, (256, 512), 1)
    c = (rm[...] + rr[...]) * F32(1.0 / VARS) + jnp.where(
        row_of(pl.program_id(0)) == lane, sl_ref[...], 0.0
    )
    p_ref[...] = nt(c, inv_ref[...], HI)


def panel(rm, rr, inv, sl):
    return pl.pallas_call(
        panel_kernel,
        grid=(4,),
        in_specs=[BLOCK] * 2 + [once(512, 512), once(1, 512)],
        out_specs=BLOCK,
        out_shape=TALL,
        compiler_params=params(24),
        cost_estimate=cost(5),
        name="panel",
    )(rm, rr, inv, sl)


def final_kernel(tm, tr, p_ref, lm, lr, inv_ref, sc_ref, out_ref, u_ref):
    k = lax.axis_index("x") * 2 + lax.axis_index("zl")
    core = lax.axis_index("core")
    scale = F32(1.0 / VARS)

    @pl.when(pl.program_id(0) == 0)
    def _():
        row = lax.broadcasted_iota(jnp.int32, (512, 512), 0)
        col = column_of(lax.broadcasted_iota(jnp.int32, (512, 512), 1))
        c = (lm[...] + lr[...]) * scale + jnp.where(row == col, sc_ref[...], 0.0)
        u_ref[...] = nn(inv_ref[...], c, HI)

    p = p_ref[...]
    col = column_of(lax.broadcasted_iota(jnp.int32, (256, 512), 1))
    c = (tm[...] + tr[...]) * scale + jnp.where(
        row_of(pl.program_id(0)) == col, sc_ref[...], 0.0
    )
    out_ref[:, 0, :] = c - nn(p, u_ref[...], HI)

    @pl.when(k == 0)
    def _():
        out_ref[:, 0, :256] = jnp.where(core == 0, p[:, :256], p[:, 256:])


def final(tm, tr, p, lm, lr, inv, sc):
    return pl.pallas_call(
        final_kernel,
        grid=(4,),
        in_specs=[BLOCK] * 3 + [once(512, 512)] * 3 + [once(1, 512)],
        out_specs=pl.BlockSpec((256, 1, 512), lambda m: (m, 0, 0)),
        out_shape=jax.ShapeDtypeStruct((1024, 1, 512), F32),
        scratch_shapes=[pltpu.VMEM((512, 512), F32)],
        compiler_params=params(32),
        cost_estimate=cost(9),
        name="final",
    )(tm, tr, p, lm, lr, inv, sc)


def shift(v, axis, by):
    n = lax.axis_size(axis)
    return lax.ppermute(v, axis, [(i, (i + by) % n) for i in range(n)])


def after(v, *others):
    return lax.optimization_barrier((v, *others))[0]


def near(v, axis):
    return shift(v, axis, -1), shift(v, axis, 1)


def body(samples, shrink):
    k = lax.axis_index("x") * 2 + lax.axis_index("zl")
    core = lax.axis_index("core")
    zz = ("zh", "zl")
    rows, up, down, lead, strip = prep(samples)
    cols = lax.all_to_all(strip, ("x", "zl"), split_axis=0, concat_axis=0, tiled=True)

    lead_z = shift(lead, "zl", 1)
    rows_z = jnp.concatenate([shift(up, zz, 1), shift(down, zz, -1)], axis=0)
    l_up, l_down = near(lead, "x")
    lead_z, l_up, l_down, cols = lax.optimization_barrier((lead_z, l_up, l_down, cols))
    lz_up, lz_down = near(lead_z, "x")
    l_far, lz_far = shift(l_down, "x", 1), shift(lz_up, "x", -1)
    cols_z = shift(cols, "zh", 1)
    b_own = lax.all_gather(cols, "y")
    b_z = lax.all_gather(cols_z, "y")
    rows = after(rows, lead_z)
    a_up, a_down = near(rows, "x")
    az_up, az_down = near(rows_z, "x")
    g, lead_all = lead_gram([lead, l_up, l_down, l_far, lead_z, lz_up, lz_down, lz_far])
    sl = shrink[:PANEL].reshape(1, PANEL)
    half_a, half_inv = chol_half(g, shift(g, "core", 1), sl)
    inv = chol_rest(half_a, half_inv)
    a_far, az_far = shift(a_down, "x", 1), shift(az_up, "x", -1)

    a = [rows, a_up, a_down, rows_z, az_up, az_down]
    own, other, rl, lc_own, lc_other, b_part = gram_first(a, lead_all, b_own, inv)
    rl = gram_middle([a_far, az_far], lead_all, rl)
    p = panel(rl, shift(rl, "core", 1), inv, sl)
    own, other, lc_own, lc_other = gram_second(
        a, [a_far, az_far], lead_all, b_z, b_part, own, other, lc_own, lc_other
    )
    sc = lax.dynamic_slice(shrink.reshape(2, 16, 256), (0, 2 * k + core, 0), (2, 1, 256))
    sc = sc.reshape(1, 512)
    out = final(own, shift(other, "core", 1), p, lc_own, shift(lc_other, "core", 1), inv, sc)
    return out.reshape(1, 1024, 1, 512)


def solution(mesh):
    fine = Mesh(mesh.devices.reshape(4, 2, 4, 2, 2), ("y", "zh", "x", "zl", "core"))
    return jax.shard_map(
        body,
        mesh=fine,
        in_specs=(P(("x", "zl", "core"), None), P()),
        out_specs=P(("y", "zh"), None, ("x", "zl", "core"), None),
        check_vma=False,
    )
```

```python
import jax
import jax.numpy as jnp
from jax import lax
from jax.experimental import pallas as pl
from jax.experimental.pallas import tpu as pltpu
from jax.sharding import Mesh, PartitionSpec as P

PANEL = 512
VARS = 8192
ROWS = 512
HI = lax.Precision.HIGHEST
F32 = jnp.float32
BF = jnp.bfloat16
MB = 1 << 20


def cost(us):
    return pl.CostEstimate(flops=us << 30, bytes_accessed=1 << 16, transcendentals=0)


ANY = pl.BlockSpec(memory_space=pl.ANY)
VM = pl.BlockSpec(memory_space=pltpu.VMEM)


def params(mb):
    return pltpu.CompilerParams(vmem_limit_bytes=mb * MB)


def nt(a, b, precision=None):
    return lax.dot_general(
        a, b, (((1,), (1,)), ((), ())), precision=precision, preferred_element_type=F32
    )


def nn(a, b, precision=None):
    return lax.dot_general(
        a, b, (((1,), (0,)), ((), ())), precision=precision, preferred_element_type=F32
    )


def prep_kernel(lo_ref, hi_ref, rows_ref, up_ref, down_ref, lead_ref, strip_ref, pick_ref):
    y, zh, zl = lax.axis_index("y"), lax.axis_index("zh"), lax.axis_index("zl")
    r = y * 2 + zh
    core = lax.axis_index("core")
    @pl.when(pl.program_id(0) == 0)
    def _():
        j = lax.broadcasted_iota(jnp.int32, (512, 128), 0)
        i = lax.broadcasted_iota(jnp.int32, (512, 128), 1)
        for h, by in enumerate((1, 3)):
            other = y * 2 + lax.rem(zh * 2 + zl + by, 4) // 2
            want = jnp.where(i < 64, r * 64 + i, other * 64 + i - 64)
            pick_ref[h] = jnp.where(j == want, 1.0, 0.0).astype(BF)

    mine = pl.ds(pl.multiple_of((zh * 4 + y) * 64, 64), 64)
    for h, (ref, out) in enumerate(((lo_ref, up_ref), (hi_ref, down_ref))):
        picked = nn(ref[...], pick_ref[h]).astype(BF).T
        rows_ref[h, 0] = picked[:64]
        out[0] = picked[64:]
        part = ref[mine, :]
        left, right = part[:, :256], part[:, 256:]
        strip_ref[0, :, h * 256 : h * 256 + 256] = jnp.where(core == 0, left, right)
        strip_ref[0, :, 512 + h * 256 : 768 + h * 256] = jnp.where(core == 0, right, left)

    @pl.when(pl.program_id(0) == 0)
    def _():
        lead_ref[...] = lo_ref[...].T


def prep(x):
    rows, up, down, lead, strip = pl.pallas_call(
        prep_kernel,
        grid=(8,),
        in_specs=[
            pl.BlockSpec((ROWS, 512), lambda k: (0, k)),
            pl.BlockSpec((ROWS, 512), lambda k: (0, k + 8)),
        ],
        out_specs=[
            pl.BlockSpec((2, 1, 64, ROWS), lambda k: (0, k, 0, 0)),
            pl.BlockSpec((1, 64, ROWS), lambda k: (k, 0, 0)),
            pl.BlockSpec((1, 64, ROWS), lambda k: (k, 0, 0)),
            pl.BlockSpec((512, ROWS), lambda k: (0, 0)),
            pl.BlockSpec((1, 64, 1024), lambda k: (k, 0, 0)),
        ],
        out_shape=[
            jax.ShapeDtypeStruct((2, 8, 64, ROWS), BF),
            jax.ShapeDtypeStruct((8, 64, ROWS), BF),
            jax.ShapeDtypeStruct((8, 64, ROWS), BF),
            jax.ShapeDtypeStruct((512, ROWS), BF),
            jax.ShapeDtypeStruct((8, 64, 1024), BF),
        ],
        scratch_shapes=[pltpu.VMEM((2, 512, 128), BF)],
        compiler_params=params(58),
        cost_estimate=cost(9),
        name="prep",
    )(x, x)
    return rows.reshape(1024, ROWS), up.reshape(512, ROWS), down.reshape(512, ROWS), lead, strip


def place(dx, dz):
    return lax.rem(lax.axis_index("x") + dx, 4) * 2 + lax.rem(lax.axis_index("zl") + dz, 2)


def lead_kernel(*refs):
    gram_ref, all_ref = refs[-2:]
    for dz in range(2):
        for n, dx in enumerate((0, 1, 3, 2)):
            all_ref[place(dx, dz)] = refs[4 * dz + n][...]
    total = None
    for k in range(8):
        v = all_ref[k]
        term = nt(v, v)
        total = term if total is None else total + term
    gram_ref[...] = total


def lead_gram(pieces):
    return pl.pallas_call(
        lead_kernel,
        in_specs=[VM] * len(pieces),
        out_specs=[VM, VM],
        out_shape=[
            jax.ShapeDtypeStruct((512, 512), F32),
            jax.ShapeDtypeStruct((8, 512, 512), BF),
        ],
        compiler_params=params(24),
        cost_estimate=cost(4),
        name="lead_gram",
    )(*pieces)


def factor128(block):
    tiles = [block[8 * t : 8 * t + 8, :] for t in range(16)]
    lane = lax.broadcasted_iota(jnp.int32, (8, 128), 1)
    sub = lax.broadcasted_iota(jnp.int32, (8, 128), 0)
    out = []
    for g in range(16):
        j0 = 8 * g
        group = (lane >= j0) & (lane < j0 + 8)
        cols = [jnp.broadcast_to(tiles[g][:, j0 + s : j0 + s + 1], (8, 128)) for s in range(8)]
        jordan = jnp.where(group, jnp.where(lane - j0 == sub, 1.0, 0.0), tiles[g])
        kept = jnp.zeros((8, 128), F32)
        invs = jnp.ones((8, 128), F32)
        for s in range(8):
            here = sub == s
            inv = 1.0 / jnp.broadcast_to(cols[s][s : s + 1, :], (8, 128))
            row = jnp.broadcast_to(jordan[s : s + 1, :], (8, 128))
            kept = jnp.where(here, row, kept)
            invs = jnp.where(here, inv, invs)
            factor = jnp.where(here, 1.0 - inv, cols[s] * inv)
            jordan = jordan - factor * row
            for q in range(s + 1, 8):
                cols[q] = cols[q] - factor * jnp.broadcast_to(cols[q][s : s + 1, :], (8, 128))
        out.append(jnp.where(lane <= sub + j0, kept * jnp.sqrt(invs), 0.0))
        for t in range(g + 1, 16):
            tile = jnp.where(group, 0.0, tiles[t])
            for s in range(8):
                tile = tile - tiles[t][:, j0 + s : j0 + s + 1] * jordan[s : s + 1, :]
            tiles[t] = tile
    return jnp.concatenate(out, axis=0)


def chol_blocks(a_ref, inv_ref, blocks):
    for b in blocks:
        lo, hi = b * 128, b * 128 + 128
        w = factor128(a_ref[lo:hi, lo:hi])
        if b > 0:
            mid = nn(a_ref[lo:hi, :lo], inv_ref[:lo, :lo], HI)
            inv_ref[lo:hi, :lo] = -nn(w, mid, HI)
        inv_ref[lo:hi, lo:hi] = w
        if b < 3:
            below = nt(a_ref[hi:, lo:hi], w, HI)
            a_ref[hi:, lo:hi] = below
            a_ref[hi:, hi:] = a_ref[hi:, hi:] - nt(below, below, HI)


def chol_first(g0, g1, shrink_ref, a_ref, inv_ref):
    i = lax.broadcasted_iota(jnp.int32, (512, 512), 0)
    j = lax.broadcasted_iota(jnp.int32, (512, 512), 1)
    a_ref[...] = (g0[...] + g1[...]) * F32(1.0 / VARS) + jnp.where(
        i == j, shrink_ref[...], 0.0
    )
    inv_ref[...] = jnp.zeros((512, 512), F32)
    chol_blocks(a_ref, inv_ref, (0, 1))


def chol_second(a0, i0, inv_ref, a_ref):
    a_ref[...] = a0[...]
    inv_ref[...] = i0[...]
    chol_blocks(a_ref, inv_ref, (2, 3))


SQUARE = jax.ShapeDtypeStruct((512, 512), F32)


def chol_half(g0, g1, shrink_lead):
    return pl.pallas_call(
        chol_first,
        in_specs=[VM] * 3,
        out_specs=[VM, VM],
        out_shape=[SQUARE, SQUARE],
        compiler_params=params(16),
        cost_estimate=cost(80),
        name="chol_first",
    )(g0, g1, shrink_lead)


def chol_rest(a, inv):
    return pl.pallas_call(
        chol_second,
        in_specs=[VM, VM],
        out_specs=VM,
        out_shape=SQUARE,
        scratch_shapes=[pltpu.VMEM((512, 512), F32)],
        compiler_params=params(16),
        cost_estimate=cost(80),
        name="chol_second",
    )(a, inv)


TALL = jax.ShapeDtypeStruct((1024, 512), F32)
NEAR = tuple((dx, dz) for dz in range(2) for dx in (0, 1, 3))
FAR = ((2, 0), (2, 1))


def fetch(b_ref, b_s, sems):
    copies = []
    for y in range(4):
        c = pltpu.make_async_copy(b_ref.at[y], b_s.at[:, y], sems.at[y])
        c.start()
        copies.append(c)
    for c in copies:
        c.wait()


def other_zh():
    return lax.rem(lax.axis_index("zh") + 1, 2)


def half_lanes(dz):
    zh = lax.rem(lax.axis_index("zh") + dz, 2)
    return pl.ds(pl.multiple_of(zh * 256, 256), 256)


def lead_products(l_ref, b_s, lanes, m):
    rows = pl.ds(pl.multiple_of(m * 256, 256), 256)
    total = None
    for k in range(8):
        term = nn(l_ref[k, rows, lanes], b_s[k].reshape(256, 1024))
        total = term if total is None else total + term
    return rows, total


def row_products(a_in, order, b_s, lanes):
    total = None
    for ref, (dx, dz) in zip(a_in, order):
        term = nn(ref[:, lanes], b_s[place(dx, dz)].reshape(256, 1024))
        total = term if total is None else total + term
    return total


def side_products(a_in, order, l_ref):
    total = None
    for ref, (dx, dz) in zip(a_in, order):
        term = nt(ref[...], l_ref[place(dx, dz)])
        total = term if total is None else total + term
    return total


def first_kernel(*refs):
    a_in, l_ref, b_ref = refs[:6], refs[6], refs[7]
    own, other, rl, lc_own, lc_other, far_ref, b_s, sems = refs[9:]
    lanes = half_lanes(0)

    @pl.when(pl.program_id(0) == 0)
    def _():
        fetch(b_ref, b_s, sems)

        def step(m, _):
            rows, total = lead_products(l_ref, b_s, lanes, m)
            lc_own[rows, :] = total[:, :512]
            lc_other[rows, :] = total[:, 512:]
            return 0

        lax.fori_loop(0, 2, step, 0)
        for dz in range(2):
            far_ref[dz] = b_s[place(2, dz)].reshape(256, 1024)

    tile = row_products(a_in, NEAR, b_s, lanes)
    own[...] = tile[:, :512]
    other[...] = tile[:, 512:]
    rl[...] = side_products(a_in, NEAR, l_ref)


def middle_kernel(a0, a1, l_ref, rl0, rl):
    rl[...] = rl0[...] + side_products((a0, a1), FAR, l_ref)


def second_kernel(*refs):
    near_in, far_in, l_ref, b_ref, far_ref = refs[:6], refs[6:8], refs[8], refs[9], refs[10]
    own0, other0, lc_own0, lc_other0 = refs[11:15]
    own, other, lc_own, lc_other, b_s, sems = refs[15:]
    half = slice(None)

    @pl.when(pl.program_id(0) == 0)
    def _():
        fetch(b_ref, b_s, sems)

        def step(m, _):
            rows, total = lead_products(l_ref, b_s, half, m)
            lc_own[rows, :] = lc_own0[rows, :] + total[:, :512]
            lc_other[rows, :] = lc_other0[rows, :] + total[:, 512:]
            return 0

        lax.fori_loop(0, 2, step, 0)

    tile = row_products(near_in, NEAR, b_s, half)
    tile = tile + row_products(far_in, FAR, b_s, half_lanes(1))
    for dz in range(2):
        tile = tile + nn(far_in[dz][:, half_lanes(0)], far_ref[dz])
    own[...] = own0[...] + tile[:, :512]
    other[...] = other0[...] + tile[:, 512:]


def once(*shape):
    return pl.BlockSpec(shape, lambda m: (0,) * len(shape))


BLOCK = pl.BlockSpec((256, 512), lambda m: (m, 0))
SCRATCH = [pltpu.VMEM((8, 4, 64, 1024), BF), pltpu.SemaphoreType.DMA((4,))]


def gram_first(a, lead, b, after):
    return pl.pallas_call(
        first_kernel,
        grid=(4,),
        in_specs=[BLOCK] * 6 + [once(8, 512, 512), ANY, ANY],
        out_specs=[BLOCK] * 3 + [once(512, 512)] * 2 + [once(2, 256, 1024)],
        out_shape=[TALL] * 3 + [SQUARE] * 2 + [jax.ShapeDtypeStruct((2, 256, 1024), BF)],
        scratch_shapes=SCRATCH,
        compiler_params=params(40),
        cost_estimate=cost(17),
        name="gram_first",
    )(*a, lead, b, after)


def gram_middle(a, lead, rl):
    return pl.pallas_call(
        middle_kernel,
        grid=(4,),
        in_specs=[BLOCK] * 2 + [once(8, 512, 512)] + [BLOCK],
        out_specs=BLOCK,
        out_shape=TALL,
        compiler_params=params(40),
        cost_estimate=cost(5),
        name="gram_middle",
    )(*a, lead, rl)


def gram_second(near_a, far_a, lead, b, b_part, own, other, lc_own, lc_other):
    return pl.pallas_call(
        second_kernel,
        grid=(4,),
        in_specs=[pl.BlockSpec((256, 256), lambda m: (m, other_zh()))] * 6
        + [BLOCK] * 2
        + [pl.BlockSpec((8, 512, 256), lambda m: (0, 0, other_zh())), ANY, once(2, 256, 1024)]
        + [BLOCK] * 2
        + [once(512, 512)] * 2,
        out_specs=[BLOCK] * 2 + [once(512, 512)] * 2,
        out_shape=[TALL] * 2 + [SQUARE] * 2,
        scratch_shapes=SCRATCH,
        compiler_params=params(58),
        cost_estimate=cost(10),
        name="gram_second",
    )(*near_a, *far_a, lead, b, b_part, own, other, lc_own, lc_other)


def column_of(lane):
    k = lax.axis_index("x") * 2 + lax.axis_index("zl")
    return (lane // 256) * 4096 + k * 512 + lax.axis_index("core") * 256 + lane % 256


def row_of(step):
    r = lax.axis_index("y") * 2 + lax.axis_index("zh")
    local = lax.broadcasted_iota(jnp.int32, (256, 512), 0) + step * 256
    return (local // 64) * 512 + r * 64 + local % 64


def panel_kernel(rm, rr, inv_ref, sl_ref, p_ref):
    lane = lax.broadcasted_iota(jnp.int32, (256, 512), 1)
    c = (rm[...] + rr[...]) * F32(1.0 / VARS) + jnp.where(
        row_of(pl.program_id(0)) == lane, sl_ref[...], 0.0
    )
    p_ref[...] = nt(c, inv_ref[...], HI)


def panel(rm, rr, inv, sl):
    return pl.pallas_call(
        panel_kernel,
        grid=(4,),
        in_specs=[BLOCK] * 2 + [once(512, 512), once(1, 512)],
        out_specs=BLOCK,
        out_shape=TALL,
        compiler_params=params(24),
        cost_estimate=cost(5),
        name="panel",
    )(rm, rr, inv, sl)


def final_kernel(tm, tr, p_ref, lm, lr, inv_ref, sc_ref, out_ref, u_ref):
    k = lax.axis_index("x") * 2 + lax.axis_index("zl")
    core = lax.axis_index("core")
    scale = F32(1.0 / VARS)

    @pl.when(pl.program_id(0) == 0)
    def _():
        row = lax.broadcasted_iota(jnp.int32, (512, 512), 0)
        col = column_of(lax.broadcasted_iota(jnp.int32, (512, 512), 1))
        c = (lm[...] + lr[...]) * scale + jnp.where(row == col, sc_ref[...], 0.0)
        u_ref[...] = nn(inv_ref[...], c, HI)

    p = p_ref[...]
    col = column_of(lax.broadcasted_iota(jnp.int32, (256, 512), 1))
    c = (tm[...] + tr[...]) * scale + jnp.where(
        row_of(pl.program_id(0)) == col, sc_ref[...], 0.0
    )
    out_ref[:, 0, :] = c - nn(p, u_ref[...], HI)

    @pl.when(k == 0)
    def _():
        out_ref[:, 0, :256] = jnp.where(core == 0, p[:, :256], p[:, 256:])


def final(tm, tr, p, lm, lr, inv, sc):
    return pl.pallas_call(
        final_kernel,
        grid=(4,),
        in_specs=[BLOCK] * 3 + [once(512, 512)] * 3 + [once(1, 512)],
        out_specs=pl.BlockSpec((256, 1, 512), lambda m: (m, 0, 0)),
        out_shape=jax.ShapeDtypeStruct((1024, 1, 512), F32),
        scratch_shapes=[pltpu.VMEM((512, 512), F32)],
        compiler_params=params(32),
        cost_estimate=cost(9),
        name="final",
    )(tm, tr, p, lm, lr, inv, sc)


def shift(v, axis, by):
    n = lax.axis_size(axis)
    return lax.ppermute(v, axis, [(i, (i + by) % n) for i in range(n)])


def after(v, *others):
    return lax.optimization_barrier((v, *others))[0]


def near(v, axis):
    return shift(v, axis, -1), shift(v, axis, 1)


def body(samples, shrink):
    k = lax.axis_index("x") * 2 + lax.axis_index("zl")
    core = lax.axis_index("core")
    zz = ("zh", "zl")
    rows, up, down, lead, strip = prep(samples)
    cols = lax.all_to_all(strip, ("x", "zl"), split_axis=0, concat_axis=0, tiled=True)

    lead_z = shift(lead, "zl", 1)
    rows_z = jnp.concatenate([shift(up, zz, 1), shift(down, zz, -1)], axis=0)
    l_up, l_down = near(lead, "x")
    lead_z, l_up, l_down, cols = lax.optimization_barrier((lead_z, l_up, l_down, cols))
    lz_up, lz_down = near(lead_z, "x")
    l_far, lz_far = shift(l_down, "x", 1), shift(lz_up, "x", -1)
    cols_z = shift(cols, "zh", 1)
    b_own = lax.all_gather(cols, "y")
    b_z = lax.all_gather(cols_z, "y")
    rows = after(rows, lead_z)
    a_up, a_down = near(rows, "x")
    az_up, az_down = near(rows_z, "x")
    g, lead_all = lead_gram([lead, l_up, l_down, l_far, lead_z, lz_up, lz_down, lz_far])
    sl = shrink[:PANEL].reshape(1, PANEL)
    half_a, half_inv = chol_half(g, shift(g, "core", 1), sl)
    inv = chol_rest(half_a, half_inv)
    a_far, az_far = shift(a_down, "x", 1), shift(az_up, "x", -1)

    a = [rows, a_up, a_down, rows_z, az_up, az_down]
    own, other, rl, lc_own, lc_other, b_part = gram_first(a, lead_all, b_own, inv)
    rl = gram_middle([a_far, az_far], lead_all, rl)
    p = panel(rl, shift(rl, "core", 1), inv, sl)
    own, other, lc_own, lc_other = gram_second(
        a, [a_far, az_far], lead_all, b_z, b_part, own, other, lc_own, lc_other
    )
    sc = lax.dynamic_slice(shrink.reshape(2, 16, 256), (0, 2 * k + core, 0), (2, 1, 256))
    sc = sc.reshape(1, 512)
    out = final(own, shift(other, "core", 1), p, lc_own, shift(lc_other, "core", 1), inv, sc)
    return out.reshape(1, 1024, 1, 512)


def solution(mesh):
    fine = Mesh(mesh.devices.reshape(4, 2, 4, 2, 2), ("y", "zh", "x", "zl", "core"))
    return jax.shard_map(
        body,
        mesh=fine,
        in_specs=(P(("x", "zl", "core"), None), P()),
        out_specs=P(("y", "zh"), None, ("x", "zl", "core"), None),
        check_vma=False,
    )
```
